512 devices in a mesh: pipe: 64 (over y, z_hi, core), tensor: 8 (over z_lo, x).
Axes of the slice: x: 4, y: 8, z: 8 (z_hi: 4, z_lo: 2; z = z_hi * 2 + z_lo), core: 2. Of those that a mesh axis runs over, the one named last changes fastest.
Arguments:
- queries: bfloat16 [64, 128, 4096], P('pipe', None, 'tensor'), may hold values from -6 to 6
- keys: bfloat16 [64, 128, 1024], P('pipe', None, 'tensor'), may hold values from -6 to 6
- values: bfloat16 [64, 128, 1024], P('pipe', None, 'tensor'), may hold values from -6 to 6
- out_grad: bfloat16 [64, 128, 4096], P('pipe', None, 'tensor'), may hold values from -18 to 18
- key_weight: bfloat16 [64, 4096, 1024], P('pipe', None, 'tensor'), may hold values from -0.09375 to 0.09375
- value_weight: bfloat16 [64, 4096, 1024], P('pipe', None, 'tensor'), may hold values from -0.09375 to 0.09375
- head_gate: float32 [64, 32], P('pipe', 'tensor'), may hold values from 0.4 to 1.2
- layer_gate: float32 [64], P('pipe'), may hold values from 0.5 to 1.5
- head_order: int32 [64, 32], P('pipe'), may hold values from 0 to 31, each once within a row
Outputs:
- input_grad: bfloat16 [64, 128, 4096], P('pipe', None, 'tensor')
- head_grad: float32 [64, 32], P('pipe', 'tensor')
- layer_grad: float32 [64], P('pipe')
The draws below stay inside these ranges and needn't reach their ends.
Inputs may be any that keep to these rules, and one draw needn't show every extreme that they name: `head_order`: the first 8 entries of each layer's row name its masked heads.
All inputs are finite; a program needn't handle non-finite values.
Results may differ from the reference program's by a relative error of at most 0.019.
Values may be sent and summed in bfloat16 or wider, within the bound.
No kernel may reach another device: no remote copies, remote signals or barrier semaphores. Data moves between devices by JAX's collectives and lax.ppermute only.
A program may use at most 64 MiB of HBM per device.

```python
import jax
import jax.numpy as jnp
from jax import lax

D = 4096
HEAD = 128
KV_HEADS = 8
Q_HEADS = 32
MASKED = 8
S = 128
SECTIONS = 64
N_TENSOR = 8


def draw_queries(key, part):
    key = jax.random.fold_in(key, 1)
    sample = jnp.clip(jax.random.normal(key, (SECTIONS, S, Q_HEADS * HEAD), jnp.float32), -6.0, 6.0)
    return sample.astype(jnp.bfloat16)


def draw_keys(key, part):
    key = jax.random.fold_in(key, 2)
    sample = jnp.clip(jax.random.normal(key, (SECTIONS, S, KV_HEADS * HEAD), jnp.float32), -6.0, 6.0)
    return sample.astype(jnp.bfloat16)


def levels(own_key, shape, split, smallest, largest):
    loudness = 1.0
    for axis_at, parts in split:
        steps = jax.random.uniform(jax.random.fold_in(jax.random.fold_in(own_key, 6), axis_at), (parts,), jnp.float32, smallest / len(split), largest / len(split))
        loudness = loudness * jnp.repeat(jnp.exp(steps), shape[axis_at] // parts).reshape((-1,) + (1,) * (len(shape) - 1 - axis_at))
    return loudness


def noise(key, extent, scale, limit, split=(), held_as=jnp.bfloat16):
    level = levels(key, extent, split, -0.22, 0.18) if split else 1.0
    result = jax.random.normal(key, extent, jnp.float32) * scale * level
    return jnp.minimum(jnp.maximum(result, -limit), limit).astype(held_as)


def setup_inputs(seed: int = 0) -> dict:
    seeds = jax.random.split(jax.random.key(seed), 10)
    return {
        "queries": draw_queries(jax.random.fold_in(seeds[9], 71), 0),
        "keys": draw_keys(jax.random.fold_in(seeds[9], 71), 0),
        "values": noise(seeds[2], (SECTIONS, S, KV_HEADS * HEAD), 1.0, 6.0, ((0, 64), (2, 8))),
        "out_grad": noise(seeds[3], (SECTIONS, S, Q_HEADS * HEAD), 3.0, 18.0, ((0, 64), (2, 8))),
        "key_weight": noise(seeds[4], (SECTIONS, D, KV_HEADS * HEAD), D ** -0.5, 0.09375, ((0, 64), (2, 8))),
        "value_weight": noise(seeds[5], (SECTIONS, D, KV_HEADS * HEAD), D ** -0.5, 0.09375, ((0, 64), (2, 8))),
        "head_gate": jnp.clip(0.4 + 0.800000042 * jax.random.uniform(seeds[6], (SECTIONS, Q_HEADS), jnp.float32) ** levels(seeds[6], (SECTIONS, Q_HEADS), ((0, 64), (1, 8)), -0.2, 0.2), 0.4, 1.2),
        "layer_gate": jnp.clip(0.5 + 1.0 * jax.random.uniform(seeds[7], (SECTIONS,), jnp.float32) ** levels(seeds[7], (SECTIONS,), ((0, 64),), -0.2, 0.2), 0.5, 1.5),
        "head_order": jax.vmap(lambda own: jax.random.permutation(own, Q_HEADS))(jax.random.split(seeds[8], SECTIONS)).reshape((SECTIONS, Q_HEADS)).astype(jnp.int32),
    }


def round_half(array):
    return lax.optimization_barrier(array.astype(jnp.bfloat16)).astype(jnp.float32)


def layer_terms(query_rows, key_rows, value_rows, grad_rows, key_proj, value_proj, gate_row, layer_value, order_row):
    group_size = Q_HEADS // KV_HEADS
    score_scale = HEAD ** -0.5
    query_heads = query_rows.reshape(S, KV_HEADS, group_size, HEAD).astype(jnp.float32)
    key_heads = key_rows.reshape(S, KV_HEADS, HEAD).astype(jnp.float32)
    value_heads = value_rows.reshape(S, KV_HEADS, HEAD).astype(jnp.float32)
    grad_heads = grad_rows.reshape(S, KV_HEADS, group_size, HEAD).astype(jnp.float32)
    scores = jnp.einsum("skgd,tkd->kgst", query_heads, key_heads) * score_scale
    row_index = jnp.arange(S, dtype=jnp.int32)[:, None]
    col_index = jnp.arange(S, dtype=jnp.int32)[None, :]
    scores = jnp.where(row_index >= col_index, scores, -1e30)
    row_max = jnp.max(scores, axis=-1, keepdims=True)
    expo = jnp.exp(scores - row_max)
    attention = expo / jnp.sum(expo, axis=-1, keepdims=True)
    probs_half = round_half(attention)
    attended = jnp.einsum("kgst,tkd->skgd", probs_half, value_heads)
    head_sum = jnp.sum(grad_heads * attended, axis=(0, 3)).reshape(Q_HEADS)
    listed = order_row[:MASKED]
    head_ids = jnp.arange(Q_HEADS, dtype=jnp.int32)
    masked = jnp.any(listed[:, None] == head_ids[None, :], axis=0)
    open_gate = gate_row * jnp.where(masked, 0.0, 1.0)
    gate_values = (layer_value * open_gate).reshape(KV_HEADS, group_size)
    scaled_grad = round_half(grad_heads * gate_values[None, :, :, None])
    prob_grad = jnp.einsum("skgd,tkd->kgst", scaled_grad, value_heads)
    centre = jnp.sum(attention * prob_grad, axis=-1, keepdims=True)
    score_grad = round_half(attention * (prob_grad - centre) * score_scale)
    key_grad = round_half(jnp.einsum("kgst,skgd->tkd", score_grad, query_heads))
    value_grad = round_half(jnp.einsum("kgst,skgd->tkd", probs_half, scaled_grad))
    local_heads = KV_HEADS // N_TENSOR
    key_grad = key_grad.reshape(S, N_TENSOR, local_heads * HEAD)
    value_grad = value_grad.reshape(S, N_TENSOR, local_heads * HEAD)
    key_split = key_proj.reshape(D, N_TENSOR, local_heads * HEAD).astype(jnp.float32)
    value_split = value_proj.reshape(D, N_TENSOR, local_heads * HEAD).astype(jnp.float32)
    group_part = jnp.einsum("sgc,dgc->gsd", key_grad, key_split) + jnp.einsum("sgc,dgc->gsd", value_grad, value_split)
    branch_grad = jnp.sum(round_half(group_part), axis=0)
    return branch_grad, layer_value * head_sum, jnp.sum(open_gate * head_sum)


def reference(queries, keys, values, out_grad, key_weight, value_weight, head_gate, layer_gate, head_order):
    def step(carry, section):
        branch_grad, head_part, layer_part = layer_terms(*section)
        total = carry + branch_grad
        return total, (total.astype(jnp.bfloat16), head_part, layer_part)

    start = jnp.zeros((S, D), jnp.float32)
    sections = (queries, keys, values, out_grad, key_weight, value_weight, head_gate, layer_gate, head_order)
    final, outputs = lax.scan(step, start, sections, reverse=True)
    return outputs[0], outputs[1], outputs[2]
```

```python
import jax
import jax.numpy as jnp
from jax import lax
from jax.experimental import pallas as pl
from jax.experimental.pallas import tpu as pltpu
from jax.sharding import PartitionSpec as P

HEAD = 128
MASKED = 8
SEQ = 128
WIDTH = 4096
HEADS_HERE = 4
PARTS = 8
SHARD = WIDTH // PARTS
EXTRA = 16
WEIGHT_COPIES = 4

LAYERS = ("y", "zh", "core")
TENSOR = ("zl", "x")
GROUP = ("zh", "core")

F32 = jnp.float32
BF16 = jnp.bfloat16


def dot(a, b, a_dim, b_dim):
    return lax.dot_general(a, b, (((a_dim,), (b_dim,)), ((), ())), preferred_element_type=F32)


def front_kernel(
    order_ref, layer_gate_ref, head_gate_ref, q_ref, k_ref, v_ref, grad_ref, kw_ref, vw_ref,
    part_ref, head_grad_ref, kw_buf, vw_buf, sems,
):
    rows = WIDTH // WEIGHT_COPIES
    copies = []
    for i in range(WEIGHT_COPIES):
        span = pl.ds(i * rows, rows)
        pair = (
            pltpu.make_async_copy(kw_ref.at[0, span], kw_buf.at[span], sems.at[0, i]),
            pltpu.make_async_copy(vw_ref.at[0, span], vw_buf.at[span], sems.at[1, i]),
        )
        for copy in pair:
            copy.start()
        copies.append(pair)

    tensor_place = lax.axis_index("zl") * 4 + lax.axis_index("x")
    layer_value = layer_gate_ref[0]
    scale = HEAD ** (-0.5)
    keys = k_ref[0]
    values = v_ref[0]
    key_at = lax.broadcasted_iota(jnp.int32, (SEQ, SEQ), 0)
    query_at = lax.broadcasted_iota(jnp.int32, (SEQ, SEQ), 1)
    seen = key_at <= query_at
    lane = lax.broadcasted_iota(jnp.int32, (1, 128), 1)

    key_grad = jnp.zeros((SEQ, HEAD), F32)
    value_grad = jnp.zeros((SEQ, HEAD), F32)
    head_grads = jnp.zeros((1, 128), F32)
    layer_part = jnp.zeros((1, 1), F32)
    for h in range(HEADS_HERE):
        head_id = tensor_place * HEADS_HERE + h
        masked = order_ref[0, 0] == head_id
        for m in range(1, MASKED):
            masked = jnp.logical_or(masked, order_ref[0, m] == head_id)
        open_gate = jnp.where(masked, 0.0, head_gate_ref[0, h])
        gate = layer_value * open_gate
        span = pl.ds(h * HEAD, HEAD)
        queries = q_ref[0, :, span]
        grads = grad_ref[0, :, span]
        scores = jnp.where(seen, dot(keys, queries, 1, 1) * scale, -1e30)
        expo = jnp.exp(scores - jnp.max(scores, axis=0, keepdims=True))
        probs = expo * (1.0 / jnp.sum(expo, axis=0, keepdims=True))
        probs_half = probs.astype(BF16)
        raw = dot(values, grads, 1, 1)
        head_sum = jnp.sum(
            jnp.sum(probs_half.astype(F32) * raw, axis=0, keepdims=True), axis=1, keepdims=True
        )
        scaled = (grads.astype(F32) * gate).astype(BF16)
        prob_grad = raw * gate
        centre = jnp.sum(probs * prob_grad, axis=0, keepdims=True)
        score_grad = (probs * (prob_grad - centre) * scale).astype(BF16)
        key_grad += dot(score_grad, queries, 1, 0)
        value_grad += dot(probs_half, scaled, 1, 0)
        head_grads += jnp.where(lane == h, layer_value * head_sum, 0.0)
        layer_part += open_gate * head_sum

    head_grad_ref[...] = head_grads[:, :HEADS_HERE]
    both = jnp.concatenate([key_grad.astype(BF16), value_grad.astype(BF16)], axis=1)
    share = jnp.broadcast_to(layer_part, (EXTRA, 128))
    high = share.astype(BF16).astype(F32)
    row = lax.broadcasted_iota(jnp.int32, (EXTRA, 128), 0)
    extra = jnp.where(row < EXTRA // 2, high, share - high).astype(BF16)
    per_copy = PARTS // WEIGHT_COPIES
    for i in range(WEIGHT_COPIES):
        for copy in copies[i]:
            copy.wait()
        for j in range(i * per_copy, (i + 1) * per_copy):
            span = pl.ds(j * SHARD, SHARD)
            weights = jnp.concatenate([kw_buf[span], vw_buf[span]], axis=1)
            part_ref[j, pl.ds(0, SHARD)] = dot(weights, both, 1, 1).astype(BF16)
            part_ref[j, pl.ds(SHARD, EXTRA)] = extra


def front(order, layer_gate, head_gate, q, k, v, grad, kw, vw):
    smem = pl.BlockSpec(memory_space=pltpu.SMEM)
    vmem = pl.BlockSpec(memory_space=pltpu.VMEM)
    hbm = pl.BlockSpec(memory_space=pl.ANY)
    return pl.pallas_call(
        front_kernel,
        name="front",
        out_shape=(
            jax.ShapeDtypeStruct((PARTS, SHARD + EXTRA, SEQ), BF16),
            jax.ShapeDtypeStruct((1, HEADS_HERE), F32),
        ),
        in_specs=[smem, smem, smem, vmem, vmem, vmem, vmem, hbm, hbm],
        out_specs=(vmem, vmem),
        scratch_shapes=[
            pltpu.VMEM((WIDTH, HEAD), BF16),
            pltpu.VMEM((WIDTH, HEAD), BF16),
            pltpu.SemaphoreType.DMA((2, WEIGHT_COPIES)),
        ],
        compiler_params=pltpu.CompilerParams(vmem_limit_bytes=24 * 1024 * 1024),
    )(order, layer_gate, head_gate, q, k, v, grad, kw, vw)


def reduce_kernel(parts_ref, term_ref, layer_grad_ref):
    total = parts_ref[0].astype(F32)
    for j in range(1, PARTS):
        total += parts_ref[j].astype(F32)
    term = total[:SHARD].T.astype(BF16)
    for r in range(PARTS):
        term_ref[r] = term[r * 16:(r + 1) * 16]
    extra = total[SHARD:]
    layer_grad_ref[0] = extra[0, 0] + extra[EXTRA // 2, 0]


def totals_kernel(terms_ref, totals_ref):
    total = terms_ref[0].astype(F32)
    for j in range(1, PARTS):
        total += terms_ref[j].astype(F32)
    total = total.astype(BF16)
    for j in range(PARTS):
        totals_ref[j] = total


def suffix_kernel(terms_ref, totals_ref, out_ref):
    place = lax.axis_index("y")
    running = jnp.zeros(terms_ref.shape[1:], F32)
    for j in range(1, PARTS):
        running += jnp.where(place < j, totals_ref[j].astype(F32), 0.0)
    for j in range(PARTS - 1, -1, -1):
        running += terms_ref[j].astype(F32)
        out_ref[j] = running.astype(BF16)


def small(kernel, name, out_shape, out_specs=None):
    vmem = pl.BlockSpec(memory_space=pltpu.VMEM)
    return pl.pallas_call(
        kernel,
        name=name,
        out_shape=out_shape,
        out_specs=vmem if out_specs is None else out_specs,
        compiler_params=pltpu.CompilerParams(vmem_limit_bytes=16 * 1024 * 1024),
    )


def body(
    queries, keys, values, out_grad, key_weight, value_weight, head_gate, layer_gate, head_order
):
    part, head_grad = front(
        head_order, layer_gate, head_gate, queries, keys, values, out_grad, key_weight, value_weight
    )
    parts = lax.all_to_all(part, TENSOR, 0, 0)
    rows = jax.ShapeDtypeStruct((PARTS, SEQ // PARTS, SHARD), BF16)
    term, layer_grad = small(
        reduce_kernel,
        "reduce_parts",
        (rows, jax.ShapeDtypeStruct((1,), F32)),
        (pl.BlockSpec(memory_space=pltpu.VMEM), pl.BlockSpec(memory_space=pltpu.SMEM)),
    )(parts)
    terms = lax.all_to_all(term, GROUP, 0, 0)
    total = small(totals_kernel, "group_totals", rows)(terms)
    totals = lax.all_to_all(total, "y", 0, 0)
    sums = small(suffix_kernel, "suffix_sums", rows)(terms, totals)
    input_grad = lax.all_to_all(sums, GROUP, 0, 0).reshape(1, SEQ, SHARD)
    return input_grad, head_grad, layer_grad


def solution(mesh):
    fine = jax.sharding.Mesh(mesh.devices.reshape(8, 4, 2, 2, 4), LAYERS + TENSOR)
    rows = P(LAYERS, None, TENSOR)
    return jax.shard_map(
        body,
        mesh=fine,
        in_specs=(rows, rows, rows, rows, rows, rows, P(LAYERS, TENSOR), P(LAYERS), P(LAYERS, None)),
        out_specs=(rows, P(LAYERS, TENSOR), P(LAYERS)),
        check_vma=False,
    )
```

```python
import jax
import jax.numpy as jnp
from jax import lax
from jax.experimental import pallas as pl
from jax.experimental.pallas import tpu as pltpu
from jax.sharding import PartitionSpec as P

HEAD = 128
MASKED = 8
SEQ = 128
WIDTH = 4096
HEADS_HERE = 4
PARTS = 8
NEAR = 4
BLOCKS = PARTS * NEAR
BLOCK = WIDTH // BLOCKS
EXTRA = 8
FAR = 4

MESH_AXES = ("yh", "yl", "zh", "core", "zl", "x")
MESH_SHAPE = (4, 2, 4, 2, 2, 4)
LAYER_AXES = ("yh", "yl", "zh", "core")
TENSOR_AXES = ("zl", "x")
NEAR_AXES = ("core", "yl")

F32 = jnp.float32
BF16 = jnp.bfloat16
MIB = 1024 * 1024


def dot(a, b, a_dim, b_dim):
    return lax.dot_general(a, b, (((a_dim,), (b_dim,)), ((), ())), preferred_element_type=F32)


def front_kernel(
    order_hbm, layer_gate_hbm, head_gate_hbm, q_hbm, k_hbm, v_hbm, grad_hbm, kw_hbm, vw_hbm,
    part_ref, head_grad_ref,
    order_ref, layer_gate_ref, head_gate_ref, q_ref, k_ref, v_ref, grad_ref, kw_ref, vw_ref, sems,
):
    pairs = (
        (k_hbm, k_ref), (q_hbm, q_ref), (v_hbm, v_ref), (grad_hbm, grad_ref),
        (order_hbm, order_ref), (layer_gate_hbm, layer_gate_ref), (head_gate_hbm, head_gate_ref),
        (kw_hbm, kw_ref), (vw_hbm, vw_ref),
    )
    copies = [
        pltpu.make_async_copy(source, target, sems.at[i])
        for i, (source, target) in enumerate(pairs)
    ]
    for copy in copies:
        copy.start()

    tensor_place = lax.axis_index("zl") * 4 + lax.axis_index("x")
    scale = HEAD ** (-0.5)
    heads = range(HEADS_HERE)
    key_at = lax.broadcasted_iota(jnp.int32, (SEQ, SEQ), 0)
    query_at = lax.broadcasted_iota(jnp.int32, (SEQ, SEQ), 1)
    seen = key_at <= query_at
    lane = lax.broadcasted_iota(jnp.int32, (1, 128), 1)

    copies[0].wait()
    copies[1].wait()
    keys = k_ref[0]
    queries = [q_ref[0, :, pl.ds(h * HEAD, HEAD)] for h in heads]
    scores = [jnp.where(seen, dot(keys, queries[h], 1, 1) * scale, -1e30) for h in heads]
    copies[2].wait()
    copies[3].wait()
    values = v_ref[0]
    grads = [grad_ref[0, :, pl.ds(h * HEAD, HEAD)] for h in heads]
    raws = [dot(values, grads[h], 1, 1) for h in heads]
    expos = [jnp.exp(scores[h] - jnp.max(scores[h], axis=0, keepdims=True)) for h in heads]
    probs = [expos[h] * (1.0 / jnp.sum(expos[h], axis=0, keepdims=True)) for h in heads]
    halves = [probs[h].astype(BF16) for h in heads]
    centres = [jnp.sum(probs[h] * raws[h], axis=0, keepdims=True) for h in heads]
    sums = [jnp.sum(halves[h].astype(F32) * raws[h], axis=0, keepdims=True) for h in heads]

    for i in range(4, 7):
        copies[i].wait()
    layer_value = layer_gate_ref[0]
    key_grad = jnp.zeros((SEQ, HEAD), F32)
    value_grad = jnp.zeros((SEQ, HEAD), F32)
    head_grads = jnp.zeros((1, 128), F32)
    layer_part = jnp.zeros((1, 1), F32)
    for h in heads:
        head_id = tensor_place * HEADS_HERE + h
        masked = order_ref[0, 0] == head_id
        for m in range(1, MASKED):
            masked = jnp.logical_or(masked, order_ref[0, m] == head_id)
        open_gate = jnp.where(masked, 0.0, head_gate_ref[0, h])
        gate = layer_value * open_gate
        scaled = (grads[h].astype(F32) * gate).astype(BF16)
        score_grad = (probs[h] * (raws[h] - centres[h]) * (gate * scale)).astype(BF16)
        key_grad += dot(score_grad, queries[h], 1, 0)
        value_grad += dot(halves[h], scaled, 1, 0)
        head_sum = jnp.sum(sums[h], axis=1, keepdims=True)
        head_grads += jnp.where(lane == h, layer_value * head_sum, 0.0)
        layer_part += open_gate * head_sum

    head_grad_ref[...] = head_grads[:, :HEADS_HERE]
    both = jnp.concatenate([key_grad.astype(BF16), value_grad.astype(BF16)], axis=1)
    share = jnp.broadcast_to(layer_part, (EXTRA, 128))
    high = share.astype(BF16).astype(F32)
    row = lax.broadcasted_iota(jnp.int32, (EXTRA, 128), 0)
    extra = jnp.where(row < EXTRA // 2, high, share - high)
    copies[7].wait()
    copies[8].wait()
    for j in range(BLOCKS):
        span = pl.ds(j * BLOCK, BLOCK)
        weights = jnp.concatenate([kw_ref[0, span], vw_ref[0, span]], axis=1)
        part_ref[j] = jnp.concatenate([dot(weights, both, 1, 1), extra], axis=0).astype(BF16)


def front(order, layer_gate, head_gate, q, k, v, grad, kw, vw):
    vmem = pl.BlockSpec(memory_space=pltpu.VMEM)
    hbm = pl.BlockSpec(memory_space=pltpu.HBM)
    return pl.pallas_call(
        front_kernel,
        name="front",
        out_shape=(
            jax.ShapeDtypeStruct((BLOCKS, BLOCK + EXTRA, SEQ), BF16),
            jax.ShapeDtypeStruct((1, HEADS_HERE), F32),
        ),
        in_specs=[hbm] * 9,
        out_specs=(vmem, vmem),
        scratch_shapes=[
            pltpu.SMEM(order.shape, jnp.int32),
            pltpu.SMEM(layer_gate.shape, F32),
            pltpu.SMEM(head_gate.shape, F32),
            pltpu.VMEM(q.shape, BF16),
            pltpu.VMEM(k.shape, BF16),
            pltpu.VMEM(v.shape, BF16),
            pltpu.VMEM(grad.shape, BF16),
            pltpu.VMEM(kw.shape, BF16),
            pltpu.VMEM(vw.shape, BF16),
            pltpu.SemaphoreType.DMA((9,)),
        ],
        compiler_params=pltpu.CompilerParams(vmem_limit_bytes=58 * MIB),
    )(order, layer_gate, head_gate, q, k, v, grad, kw, vw)


def terms_kernel(parts_ref, terms_ref, totals_ref, layer_grad_ref):
    own = lax.axis_index("core") * 2 + lax.axis_index("yl")
    total = jnp.zeros((BLOCK, SEQ), F32)
    share = jnp.zeros((EXTRA, SEQ), F32)
    for n in range(NEAR):
        term = parts_ref[n].astype(F32)
        for t in range(1, PARTS):
            term += parts_ref[t * NEAR + n].astype(F32)
        terms_ref[n] = term[:BLOCK]
        total += term[:BLOCK]
        share += jnp.where(own == n, term[BLOCK:], 0.0)
    total = total.astype(BF16)
    for f in range(FAR):
        totals_ref[f] = total
    layer_grad_ref[0] = share[0, 0] + share[EXTRA // 2, 0]


def later_kernel(terms_ref, totals_ref, later_ref):
    y_place = lax.axis_index("yh")
    z_place = lax.axis_index("zh")
    far = jnp.zeros((BLOCK, SEQ), F32)
    for f in range(1, FAR):
        far += jnp.where(y_place < f, totals_ref[f].astype(F32), 0.0)
    first = terms_ref[0] + terms_ref[2]
    second = terms_ref[1] + terms_ref[3]
    for f in range(FAR):
        ahead = z_place > f
        later_ref[f, 0] = (far + second + jnp.where(ahead, first, 0.0)).astype(BF16)
        later_ref[f, 1] = (far + jnp.where(ahead, second, 0.0)).astype(BF16)


def sums_kernel(terms_ref, later_ref, sums_ref):
    for half in range(2):
        running = later_ref[0, half].astype(F32)
        for f in range(1, FAR):
            running += later_ref[f, half].astype(F32)
        for n in (2 + half, half):
            running += terms_ref[n]
            sums_ref[n] = running.T.astype(BF16)


def join_kernel(blocks_ref, out_ref):
    for n in range(NEAR):
        out_ref[0, :, n * BLOCK:(n + 1) * BLOCK] = blocks_ref[n]


def small(kernel, name, out_shape, out_specs=None):
    vmem = pl.BlockSpec(memory_space=pltpu.VMEM)
    return pl.pallas_call(
        kernel,
        name=name,
        out_shape=out_shape,
        out_specs=vmem if out_specs is None else out_specs,
        compiler_params=pltpu.CompilerParams(vmem_limit_bytes=16 * MIB),
    )


def body(
    queries, keys, values, out_grad, key_weight, value_weight, head_gate, layer_gate, head_order
):
    part, head_grad = front(
        head_order, layer_gate, head_gate, queries, keys, values, out_grad, key_weight, value_weight
    )
    parts = lax.all_to_all(part, TENSOR_AXES + NEAR_AXES, 0, 0)
    vmem = pl.BlockSpec(memory_space=pltpu.VMEM)
    terms, totals, layer_grad = small(
        terms_kernel,
        "terms",
        (
            jax.ShapeDtypeStruct((NEAR, BLOCK, SEQ), F32),
            jax.ShapeDtypeStruct((FAR, BLOCK, SEQ), BF16),
            jax.ShapeDtypeStruct((1,), F32),
        ),
        (vmem, vmem, pl.BlockSpec(memory_space=pltpu.SMEM)),
    )(parts)
    totals = lax.all_to_all(totals, "yh", 0, 0)
    later = small(
        later_kernel, "later", jax.ShapeDtypeStruct((FAR, 2, BLOCK, SEQ), BF16)
    )(terms, totals)
    later = lax.all_to_all(later, "zh", 0, 0)
    sums = small(
        sums_kernel, "sums", jax.ShapeDtypeStruct((NEAR, SEQ, BLOCK), BF16)
    )(terms, later)
    sums = lax.all_to_all(sums, NEAR_AXES, 0, 0)
    input_grad = small(
        join_kernel, "join", jax.ShapeDtypeStruct((1, SEQ, NEAR * BLOCK), BF16)
    )(sums)
    return input_grad, head_grad, layer_grad


def solution(mesh):
    fine = jax.sharding.Mesh(mesh.devices.reshape(MESH_SHAPE), MESH_AXES)
    rows = P(LAYER_AXES, None, TENSOR_AXES)
    heads = P(LAYER_AXES, TENSOR_AXES)
    layers = P(LAYER_AXES)
    return jax.shard_map(
        body,
        mesh=fine,
        in_specs=(rows, rows, rows, rows, rows, rows, heads, layers, P(LAYER_AXES, None)),
        out_specs=(rows, heads, layers),
        check_vma=False,
    )
```

```python
import jax
import jax.numpy as jnp
from jax import lax
from jax.experimental import pallas as pl
from jax.experimental.pallas import tpu as pltpu
from jax.sharding import PartitionSpec as P

HEAD = 128
MASKED = 8
SEQ = 128
WIDTH = 4096
HEADS_HERE = 4
PARTS = 8
NEAR = 4
BLOCKS = PARTS * NEAR
BLOCK = WIDTH // BLOCKS
EXTRA = 8
FAR = 4

MESH_AXES = ("yh", "yl", "zh", "core", "zl", "x")
MESH_SHAPE = (4, 2, 4, 2, 2, 4)
LAYER_AXES = ("yh", "yl", "zh", "core")
TENSOR_AXES = ("zl", "x")
NEAR_AXES = ("core", "yl")

F32 = jnp.float32
BF16 = jnp.bfloat16
MIB = 1024 * 1024


def dot(a, b, a_dim, b_dim):
    return lax.dot_general(a, b, (((a_dim,), (b_dim,)), ((), ())), preferred_element_type=F32)


def front_kernel(
    order_hbm, head_gate_hbm, q_hbm, k_hbm, v_hbm, grad_hbm, kw_hbm, vw_hbm,
    part_ref, head_sum_ref,
    order_ref, head_gate_ref, q_ref, k_ref, v_ref, grad_ref, kw_ref, vw_ref, sems,
):
    pairs = (
        (k_hbm, k_ref), (q_hbm, q_ref), (v_hbm, v_ref), (grad_hbm, grad_ref),
        (order_hbm, order_ref), (head_gate_hbm, head_gate_ref),
        (kw_hbm, kw_ref), (vw_hbm, vw_ref),
    )
    copies = [
        pltpu.make_async_copy(source, target, sems.at[i])
        for i, (source, target) in enumerate(pairs)
    ]
    for copy in copies:
        copy.start()

    tensor_place = lax.axis_index("zl") * 4 + lax.axis_index("x")
    scale = HEAD ** (-0.5)
    heads = range(HEADS_HERE)
    key_at = lax.broadcasted_iota(jnp.int32, (SEQ, SEQ), 0)
    query_at = lax.broadcasted_iota(jnp.int32, (SEQ, SEQ), 1)
    seen = key_at <= query_at
    lane = lax.broadcasted_iota(jnp.int32, (1, 128), 1)

    copies[0].wait()
    copies[1].wait()
    keys = k_ref[0]
    queries = [q_ref[0, :, pl.ds(h * HEAD, HEAD)] for h in heads]
    scores = [jnp.where(seen, dot(keys, queries[h], 1, 1) * scale, -1e30) for h in heads]
    copies[2].wait()
    copies[3].wait()
    values = v_ref[0]
    grads = [grad_ref[0, :, pl.ds(h * HEAD, HEAD)] for h in heads]
    raws = [dot(values, grads[h], 1, 1) for h in heads]
    expos = [jnp.exp(scores[h] - jnp.max(scores[h], axis=0, keepdims=True)) for h in heads]
    probs = [expos[h] * (1.0 / jnp.sum(expos[h], axis=0, keepdims=True)) for h in heads]
    halves = [probs[h].astype(BF16) for h in heads]
    centres = [jnp.sum(probs[h] * raws[h], axis=0, keepdims=True) for h in heads]
    sums = [jnp.sum(halves[h].astype(F32) * raws[h], axis=0, keepdims=True) for h in heads]

    for i in range(4, 6):
        copies[i].wait()
    key_grad = jnp.zeros((SEQ, HEAD), F32)
    value_grad = jnp.zeros((SEQ, HEAD), F32)
    head_sums = jnp.zeros((1, 128), F32)
    layer_part = jnp.zeros((1, 1), F32)
    for h in heads:
        head_id = tensor_place * HEADS_HERE + h
        masked = order_ref[0, 0] == head_id
        for m in range(1, MASKED):
            masked = jnp.logical_or(masked, order_ref[0, m] == head_id)
        open_gate = jnp.where(masked, 0.0, head_gate_ref[0, h])
        scaled = (grads[h].astype(F32) * open_gate).astype(BF16)
        score_grad = (probs[h] * (raws[h] - centres[h]) * (open_gate * scale)).astype(BF16)
        key_grad += dot(score_grad, queries[h], 1, 0)
        value_grad += dot(halves[h], scaled, 1, 0)
        head_sum = jnp.sum(sums[h], axis=1, keepdims=True)
        head_sums += jnp.where(lane == h, head_sum, 0.0)
        layer_part += open_gate * head_sum

    head_sum_ref[...] = head_sums
    both = jnp.concatenate([key_grad.astype(BF16), value_grad.astype(BF16)], axis=1)
    share = jnp.broadcast_to(layer_part, (EXTRA, 128))
    high = share.astype(BF16).astype(F32)
    row = lax.broadcasted_iota(jnp.int32, (EXTRA, 128), 0)
    extra = jnp.where(row < EXTRA // 2, high, share - high)
    copies[6].wait()
    copies[7].wait()
    for j in range(BLOCKS):
        span = pl.ds(j * BLOCK, BLOCK)
        weights = jnp.concatenate([kw_ref[0, span], vw_ref[0, span]], axis=1)
        part_ref[j] = jnp.concatenate([dot(weights, both, 1, 1), extra], axis=0).astype(BF16)


def front(order, head_gate, q, k, v, grad, kw, vw):
    vmem = pl.BlockSpec(memory_space=pltpu.VMEM)
    hbm = pl.BlockSpec(memory_space=pltpu.HBM)
    return pl.pallas_call(
        front_kernel,
        name="front",
        out_shape=(
            jax.ShapeDtypeStruct((BLOCKS, BLOCK + EXTRA, SEQ), BF16),
            jax.ShapeDtypeStruct((1, 128), F32),
        ),
        in_specs=[hbm] * 8,
        out_specs=(vmem, vmem),
        scratch_shapes=[
            pltpu.SMEM(order.shape, jnp.int32),
            pltpu.SMEM(head_gate.shape, F32),
            pltpu.VMEM(q.shape, BF16),
            pltpu.VMEM(k.shape, BF16),
            pltpu.VMEM(v.shape, BF16),
            pltpu.VMEM(grad.shape, BF16),
            pltpu.VMEM(kw.shape, BF16),
            pltpu.VMEM(vw.shape, BF16),
            pltpu.SemaphoreType.DMA((8,)),
        ],
        compiler_params=pltpu.CompilerParams(vmem_limit_bytes=58 * MIB),
    )(order, head_gate, q, k, v, grad, kw, vw)


def terms_kernel(parts_ref, own_gate_ref, y_gate_ref, core_gate_ref, both_gate_ref, terms_ref, totals_ref, share_ref):
    own = lax.axis_index("core") * 2 + lax.axis_index("yl")
    total = jnp.zeros((BLOCK, SEQ), F32)
    share = jnp.zeros((EXTRA, SEQ), F32)
    for n in range(NEAR):
        term = parts_ref[n].astype(F32)
        for t in range(1, PARTS):
            term += parts_ref[t * NEAR + n].astype(F32)
        apart = own ^ n
        gate = jnp.where(
            apart == 0,
            own_gate_ref[...],
            jnp.where(
                apart == 1,
                y_gate_ref[...],
                jnp.where(apart == 2, core_gate_ref[...], both_gate_ref[...]),
            ),
        )
        scaled = term[:BLOCK] * gate[:1]
        terms_ref[n] = scaled
        total += scaled
        share += jnp.where(own == n, term[BLOCK:], 0.0)
    totals_ref[...] = total.astype(BF16)
    share_ref[...] = share


def later_kernel(terms_ref, far_1, far_2, far_3, later_ref):
    z_place = lax.axis_index("zh")
    far = far_1[...].astype(F32) + far_2[...].astype(F32) + far_3[...].astype(F32)
    first = terms_ref[0] + terms_ref[2]
    second = terms_ref[1] + terms_ref[3]
    for f in range(FAR):
        ahead = z_place > f
        later_ref[f, 0] = (far + second + jnp.where(ahead, first, 0.0)).astype(BF16)
        later_ref[f, 1] = (far + jnp.where(ahead, second, 0.0)).astype(BF16)


def sums_kernel(terms_ref, later_ref, sums_ref):
    for half in range(2):
        running = later_ref[0, half].astype(F32)
        for f in range(1, FAR):
            running += later_ref[f, half].astype(F32)
        for n in (2 + half, half):
            running += terms_ref[n]
            sums_ref[n] = running.T.astype(BF16)


def join_kernel(blocks_ref, share_ref, gate_ref, head_sum_ref, out_ref, head_grad_ref, layer_grad_ref):
    head_grad_ref[...] = (gate_ref[:1] * head_sum_ref[...])[:, :HEADS_HERE]
    layer_grad_ref[0] = share_ref[0, 0] + share_ref[EXTRA // 2, 0]
    for n in range(NEAR):
        out_ref[0, :, n * BLOCK:(n + 1) * BLOCK] = blocks_ref[n]


def small(kernel, name, out_shape, out_specs=None):
    vmem = pl.BlockSpec(memory_space=pltpu.VMEM)
    return pl.pallas_call(
        kernel,
        name=name,
        out_shape=out_shape,
        out_specs=vmem if out_specs is None else out_specs,
        compiler_params=pltpu.CompilerParams(vmem_limit_bytes=16 * MIB),
    )


def body(
    queries, keys, values, out_grad, key_weight, value_weight, head_gate, layer_gate, head_order
):
    part, head_sum = front(
        head_order, head_gate, queries, keys, values, out_grad, key_weight, value_weight
    )
    part, layer_gate = lax.optimization_barrier((part, layer_gate))
    parts = lax.all_to_all(part, TENSOR_AXES + NEAR_AXES, 0, 0)
    gate = jnp.broadcast_to(layer_gate[:, None], (EXTRA, SEQ))
    swap = ((0, 1), (1, 0))
    core_gate = lax.ppermute(gate, "core", swap)
    y_gate = lax.ppermute(gate, "yl", swap)
    both_gate = lax.ppermute(core_gate, "yl", swap)
    vmem = pl.BlockSpec(memory_space=pltpu.VMEM)
    terms, totals, share = small(
        terms_kernel,
        "terms",
        (
            jax.ShapeDtypeStruct((NEAR, BLOCK, SEQ), F32),
            jax.ShapeDtypeStruct((BLOCK, SEQ), BF16),
            jax.ShapeDtypeStruct((EXTRA, SEQ), F32),
        ),
        (vmem, vmem, vmem),
    )(parts, gate, y_gate, core_gate, both_gate)
    totals = [
        lax.ppermute(totals, "yh", [(f, f - step) for f in range(step, FAR)]) for step in (3, 2, 1)
    ]
    later = small(
        later_kernel, "later", jax.ShapeDtypeStruct((FAR, 2, BLOCK, SEQ), BF16)
    )(terms, *totals)
    later = lax.all_to_all(later, "zh", 0, 0)
    sums = small(
        sums_kernel, "sums", jax.ShapeDtypeStruct((NEAR, SEQ, BLOCK), BF16)
    )(terms, later)
    sums = lax.all_to_all(sums, NEAR_AXES, 0, 0)
    input_grad, head_grad, layer_grad = small(
        join_kernel,
        "join",
        (
            jax.ShapeDtypeStruct((1, SEQ, NEAR * BLOCK), BF16),
            jax.ShapeDtypeStruct((1, HEADS_HERE), F32),
            jax.ShapeDtypeStruct((1,), F32),
        ),
        (vmem, vmem, pl.BlockSpec(memory_space=pltpu.SMEM)),
    )(sums, share, gate, head_sum)
    return input_grad, head_grad, layer_grad


def solution(mesh):
    fine = jax.sharding.Mesh(mesh.devices.reshape(MESH_SHAPE), MESH_AXES)
    rows = P(LAYER_AXES, None, TENSOR_AXES)
    heads = P(LAYER_AXES, TENSOR_AXES)
    layers = P(LAYER_AXES)
    return jax.shard_map(
        body,
        mesh=fine,
        in_specs=(rows, rows, rows, rows, rows, rows, heads, layers, P(LAYER_AXES, None)),
        out_specs=(rows, heads, layers),
        check_vma=False,
    )
```

```python
import jax
import jax.numpy as jnp
from jax import lax
from jax.experimental import pallas as pl
from jax.experimental.pallas import tpu as pltpu
from jax.sharding import PartitionSpec as P

HEAD = 128
MASKED = 8
SEQ = 128
WIDTH = 4096
HEADS_HERE = 4
PARTS = 8
NEAR = 4
BLOCKS = PARTS * NEAR
BLOCK = WIDTH // BLOCKS
EXTRA = 8
FAR = 4
STEP_1 = ((3, 0), (2, 1))
STEP_2 = ((2, 0), (3, 1))
STEP_3 = ((0, 1), (1, 0))
STEP_4 = ((1, 2), (2, 3))
STEP_5 = ((3, 2), (1, 3))
STEP_6 = ((0, 3),)

MESH_AXES = ("yh", "yl", "zh", "core", "zl", "x")
MESH_SHAPE = (4, 2, 4, 2, 2, 4)
LAYER_AXES = ("yh", "yl", "zh", "core")
TENSOR_AXES = ("zl", "x")
NEAR_AXES = ("core", "yl")

F32 = jnp.float32
BF16 = jnp.bfloat16
MIB = 1024 * 1024


def dot(a, b, a_dim, b_dim):
    return lax.dot_general(a, b, (((a_dim,), (b_dim,)), ((), ())), preferred_element_type=F32)


def front_kernel(
    order_hbm, head_gate_hbm, q_hbm, k_hbm, v_hbm, grad_hbm, kw_hbm, vw_hbm,
    part_ref, head_sum_ref,
    order_ref, head_gate_ref, q_ref, k_ref, v_ref, grad_ref, kw_ref, vw_ref, sems,
):
    pairs = (
        (k_hbm, k_ref), (q_hbm, q_ref), (v_hbm, v_ref), (grad_hbm, grad_ref),
        (order_hbm, order_ref), (head_gate_hbm, head_gate_ref),
        (kw_hbm, kw_ref), (vw_hbm, vw_ref),
    )
    copies = [
        pltpu.make_async_copy(source, target, sems.at[i])
        for i, (source, target) in enumerate(pairs)
    ]
    for copy in copies:
        copy.start()

    tensor_place = lax.axis_index("zl") * 4 + lax.axis_index("x")
    scale = HEAD ** (-0.5)
    heads = range(HEADS_HERE)
    key_at = lax.broadcasted_iota(jnp.int32, (SEQ, SEQ), 0)
    query_at = lax.broadcasted_iota(jnp.int32, (SEQ, SEQ), 1)
    seen = key_at <= query_at
    lane = lax.broadcasted_iota(jnp.int32, (1, 128), 1)

    copies[0].wait()
    copies[1].wait()
    keys = k_ref[0]
    queries = [q_ref[0, :, pl.ds(h * HEAD, HEAD)] for h in heads]
    scores = [jnp.where(seen, dot(keys, queries[h], 1, 1) * scale, -1e30) for h in heads]
    copies[2].wait()
    copies[3].wait()
    values = v_ref[0]
    grads = [grad_ref[0, :, pl.ds(h * HEAD, HEAD)] for h in heads]
    raws = [dot(values, grads[h], 1, 1) for h in heads]
    expos = [jnp.exp(scores[h] - jnp.max(scores[h], axis=0, keepdims=True)) for h in heads]
    probs = [expos[h] * (1.0 / jnp.sum(expos[h], axis=0, keepdims=True)) for h in heads]
    halves = [probs[h].astype(BF16) for h in heads]
    centres = [jnp.sum(probs[h] * raws[h], axis=0, keepdims=True) for h in heads]
    sums = [jnp.sum(halves[h].astype(F32) * raws[h], axis=0, keepdims=True) for h in heads]

    for i in range(4, 6):
        copies[i].wait()
    key_grad = jnp.zeros((SEQ, HEAD), F32)
    value_grad = jnp.zeros((SEQ, HEAD), F32)
    head_sums = jnp.zeros((1, 128), F32)
    layer_part = jnp.zeros((1, 1), F32)
    for h in heads:
        head_id = tensor_place * HEADS_HERE + h
        masked = order_ref[0, 0] == head_id
        for m in range(1, MASKED):
            masked = jnp.logical_or(masked, order_ref[0, m] == head_id)
        open_gate = jnp.where(masked, 0.0, head_gate_ref[0, h])
        scaled = (grads[h].astype(F32) * open_gate).astype(BF16)
        score_grad = (probs[h] * (raws[h] - centres[h]) * (open_gate * scale)).astype(BF16)
        key_grad += dot(score_grad, queries[h], 1, 0)
        value_grad += dot(halves[h], scaled, 1, 0)
        head_sum = jnp.sum(sums[h], axis=1, keepdims=True)
        head_sums += jnp.where(lane == h, head_sum, 0.0)
        layer_part += open_gate * head_sum

    head_sum_ref[...] = head_sums
    both = jnp.concatenate([key_grad.astype(BF16), value_grad.astype(BF16)], axis=1)
    share = jnp.broadcast_to(layer_part, (EXTRA, 128))
    high = share.astype(BF16).astype(F32)
    row = lax.broadcasted_iota(jnp.int32, (EXTRA, 128), 0)
    extra = jnp.where(row < EXTRA // 2, high, share - high)
    copies[6].wait()
    copies[7].wait()
    for j in range(BLOCKS):
        span = pl.ds(j * BLOCK, BLOCK)
        weights = jnp.concatenate([kw_ref[0, span], vw_ref[0, span]], axis=1)
        part_ref[j] = jnp.concatenate([dot(weights, both, 1, 1), extra], axis=0).astype(BF16)


def front(order, head_gate, q, k, v, grad, kw, vw):
    vmem = pl.BlockSpec(memory_space=pltpu.VMEM)
    hbm = pl.BlockSpec(memory_space=pltpu.HBM)
    return pl.pallas_call(
        front_kernel,
        name="front",
        out_shape=(
            jax.ShapeDtypeStruct((BLOCKS, BLOCK + EXTRA, SEQ), BF16),
            jax.ShapeDtypeStruct((1, 128), F32),
        ),
        in_specs=[hbm] * 8,
        out_specs=(vmem, vmem),
        scratch_shapes=[
            pltpu.SMEM(order.shape, jnp.int32),
            pltpu.SMEM(head_gate.shape, F32),
            pltpu.VMEM(q.shape, BF16),
            pltpu.VMEM(k.shape, BF16),
            pltpu.VMEM(v.shape, BF16),
            pltpu.VMEM(grad.shape, BF16),
            pltpu.VMEM(kw.shape, BF16),
            pltpu.VMEM(vw.shape, BF16),
            pltpu.SemaphoreType.DMA((8,)),
        ],
        compiler_params=pltpu.CompilerParams(vmem_limit_bytes=58 * MIB),
    )(order, head_gate, q, k, v, grad, kw, vw)


def terms_kernel(parts_ref, own_gate_ref, y_gate_ref, core_gate_ref, both_gate_ref, terms_ref, totals_ref, share_ref):
    own = lax.axis_index("core") * 2 + lax.axis_index("yl")
    total = jnp.zeros((BLOCK, SEQ), F32)
    share = jnp.zeros((EXTRA, SEQ), F32)
    for n in range(NEAR):
        term = parts_ref[n].astype(F32)
        for t in range(1, PARTS):
            term += parts_ref[t * NEAR + n].astype(F32)
        apart = own ^ n
        gate = jnp.where(
            apart == 0,
            own_gate_ref[...],
            jnp.where(
                apart == 1,
                y_gate_ref[...],
                jnp.where(apart == 2, core_gate_ref[...], both_gate_ref[...]),
            ),
        )
        scaled = term[:BLOCK] * gate[:1]
        terms_ref[n] = scaled
        total += scaled
        share += jnp.where(own == n, term[BLOCK:], 0.0)
    totals_ref[...] = total.astype(BF16)
    share_ref[...] = share


def later_kernel(
    terms_ref, far_1, far_2, far_3, own_ref, to_earlier_ref, first_later_ref, second_later_ref
):
    place = lax.axis_index("zh")
    far = far_1[...].astype(F32) + far_2[...].astype(F32) + far_3[...].astype(F32)
    first = terms_ref[0] + terms_ref[2]
    second = terms_ref[1] + terms_ref[3]
    to_later = (far + second, far)
    to_earlier = (far + second + first, far + second)
    for half in range(2):
        own_ref[half] = to_later[half]
        to_earlier_ref[half] = to_earlier[half].astype(BF16)
        for z, ref in ((0, first_later_ref), (1, second_later_ref)):
            ref[half] = jnp.where(place == z, to_later[half], to_earlier[half]).astype(BF16)


def pass_on_kernel(own_ref, step_1, step_2, step_3, sum_ref, passed_ref):
    second_place = lax.axis_index("zh") == 1
    own = own_ref[...]
    got = step_3[...].astype(F32)
    passed_ref[...] = (own + jnp.where(second_place, got, 0.0)).astype(BF16)
    sum_ref[...] = own + got + step_1[...].astype(F32) + step_2[...].astype(F32)


def sums_kernel(terms_ref, sum_ref, step_5, step_6, step_4, sums_ref):
    for half in range(2):
        running = sum_ref[half] + step_5[half].astype(F32)
        running += step_6[half].astype(F32) + step_4[half].astype(F32)
        for n in (2 + half, half):
            running += terms_ref[n]
            sums_ref[n] = running.T.astype(BF16)


def join_kernel(blocks_ref, share_ref, gate_ref, head_sum_ref, out_ref, head_grad_ref, layer_grad_ref):
    head_grad_ref[...] = (gate_ref[:1] * head_sum_ref[...])[:, :HEADS_HERE]
    layer_grad_ref[0] = share_ref[0, 0] + share_ref[EXTRA // 2, 0]
    for n in range(NEAR):
        out_ref[0, :, n * BLOCK:(n + 1) * BLOCK] = blocks_ref[n]


def small(kernel, name, out_shape, out_specs=None):
    vmem = pl.BlockSpec(memory_space=pltpu.VMEM)
    return pl.pallas_call(
        kernel,
        name=name,
        out_shape=out_shape,
        out_specs=vmem if out_specs is None else out_specs,
        compiler_params=pltpu.CompilerParams(vmem_limit_bytes=16 * MIB),
    )


def body(
    queries, keys, values, out_grad, key_weight, value_weight, head_gate, layer_gate, head_order
):
    part, head_sum = front(
        head_order, head_gate, queries, keys, values, out_grad, key_weight, value_weight
    )
    part, layer_gate = lax.optimization_barrier((part, layer_gate))
    parts = lax.all_to_all(part, TENSOR_AXES + NEAR_AXES, 0, 0)
    gate = jnp.broadcast_to(layer_gate[:, None], (EXTRA, SEQ))
    swap = ((0, 1), (1, 0))
    core_gate = lax.ppermute(gate, "core", swap)
    y_gate = lax.ppermute(gate, "yl", swap)
    both_gate = lax.ppermute(core_gate, "yl", swap)
    vmem = pl.BlockSpec(memory_space=pltpu.VMEM)
    terms, totals, share = small(
        terms_kernel,
        "terms",
        (
            jax.ShapeDtypeStruct((NEAR, BLOCK, SEQ), F32),
            jax.ShapeDtypeStruct((BLOCK, SEQ), BF16),
            jax.ShapeDtypeStruct((EXTRA, SEQ), F32),
        ),
        (vmem, vmem, vmem),
    )(parts, gate, y_gate, core_gate, both_gate)
    totals = [
        lax.ppermute(totals, "yh", [(f, f - step) for f in range(step, FAR)]) for step in (3, 2, 1)
    ]
    half_pair = (2, BLOCK, SEQ)
    own, to_earlier, first_later, second_later = small(
        later_kernel,
        "later",
        (
            jax.ShapeDtypeStruct(half_pair, F32),
            jax.ShapeDtypeStruct(half_pair, BF16),
            jax.ShapeDtypeStruct(half_pair, BF16),
            jax.ShapeDtypeStruct(half_pair, BF16),
        ),
        (vmem,) * 4,
    )(terms, *totals)
    step_1 = lax.ppermute(to_earlier, "zh", STEP_1)
    step_2 = lax.ppermute(to_earlier, "zh", STEP_2)
    step_3 = lax.ppermute(first_later, "zh", STEP_3)
    own, passed = small(
        pass_on_kernel,
        "pass_on",
        (jax.ShapeDtypeStruct(half_pair, F32), jax.ShapeDtypeStruct(half_pair, BF16)),
        (vmem,) * 2,
    )(own, step_1, step_2, step_3)
    step_5 = lax.ppermute(second_later, "zh", STEP_5)
    step_6 = lax.ppermute(first_later, "zh", STEP_6)
    step_4 = lax.ppermute(passed, "zh", STEP_4)
    sums = small(
        sums_kernel, "sums", jax.ShapeDtypeStruct((NEAR, SEQ, BLOCK), BF16)
    )(terms, own, step_5, step_6, step_4)
    sums = lax.all_to_all(sums, NEAR_AXES, 0, 0)
    input_grad, head_grad, layer_grad = small(
        join_kernel,
        "join",
        (
            jax.ShapeDtypeStruct((1, SEQ, NEAR * BLOCK), BF16),
            jax.ShapeDtypeStruct((1, HEADS_HERE), F32),
            jax.ShapeDtypeStruct((1,), F32),
        ),
        (vmem, vmem, pl.BlockSpec(memory_space=pltpu.SMEM)),
    )(sums, share, gate, head_sum)
    return input_grad, head_grad, layer_grad


def solution(mesh):
    fine = jax.sharding.Mesh(mesh.devices.reshape(MESH_SHAPE), MESH_AXES)
    rows = P(LAYER_AXES, None, TENSOR_AXES)
    heads = P(LAYER_AXES, TENSOR_AXES)
    layers = P(LAYER_AXES)
    return jax.shard_map(
        body,
        mesh=fine,
        in_specs=(rows, rows, rows, rows, rows, rows, heads, layers, P(LAYER_AXES, None)),
        out_specs=(rows, heads, layers),
        check_vma=False,
    )
```

```python
import jax
import jax.numpy as jnp
from jax import lax
from jax.experimental import pallas as pl
from jax.experimental.pallas import tpu as pltpu
from jax.sharding import PartitionSpec as P

HEAD = 128
MASKED = 8
SEQ = 128
WIDTH = 4096
HEADS_HERE = 4
PARTS = 8
NEAR = 4
BLOCKS = PARTS * NEAR
BLOCK = WIDTH // BLOCKS
EXTRA = 8
FAR = 4
STEP_1 = ((3, 0), (2, 1))
STEP_2 = ((2, 0), (3, 1))
STEP_3 = ((0, 1), (1, 0))
STEP_4 = ((1, 2), (2, 3))
STEP_5 = ((3, 2), (1, 3))
STEP_6 = ((0, 3),)

MESH_AXES = ("yh", "yl", "zh", "core", "zl", "x")
MESH_SHAPE = (4, 2, 4, 2, 2, 4)
LAYER_AXES = ("yh", "yl", "zh", "core")
TENSOR_AXES = ("zl", "x")
NEAR_AXES = ("core", "yl")

F32 = jnp.float32
BF16 = jnp.bfloat16
MIB = 1024 * 1024


def dot(a, b, a_dim, b_dim):
    return lax.dot_general(a, b, (((a_dim,), (b_dim,)), ((), ())), preferred_element_type=F32)


def front_kernel(
    order_hbm, head_gate_hbm, q_hbm, k_hbm, v_hbm, grad_hbm, kw_hbm, vw_hbm,
    part_ref, head_sum_ref,
    order_ref, head_gate_ref, q_ref, k_ref, v_ref, grad_ref, kw_ref, vw_ref, sems,
):
    pairs = (
        (k_hbm, k_ref), (q_hbm, q_ref), (v_hbm, v_ref), (grad_hbm, grad_ref),
        (order_hbm, order_ref), (head_gate_hbm, head_gate_ref),
        (kw_hbm, kw_ref), (vw_hbm, vw_ref),
    )
    copies = [
        pltpu.make_async_copy(source, target, sems.at[i])
        for i, (source, target) in enumerate(pairs)
    ]
    for copy in copies:
        copy.start()

    tensor_place = lax.axis_index("zl") * 4 + lax.axis_index("x")
    scale = HEAD ** (-0.5)
    heads = range(HEADS_HERE)
    key_at = lax.broadcasted_iota(jnp.int32, (SEQ, SEQ), 0)
    query_at = lax.broadcasted_iota(jnp.int32, (SEQ, SEQ), 1)
    seen = key_at <= query_at
    lane = lax.broadcasted_iota(jnp.int32, (1, 128), 1)

    copies[0].wait()
    copies[1].wait()
    keys = k_ref[0]
    queries = [q_ref[0, :, pl.ds(h * HEAD, HEAD)] for h in heads]
    scores = [jnp.where(seen, dot(keys, queries[h], 1, 1) * scale, -1e30) for h in heads]
    copies[2].wait()
    copies[3].wait()
    values = v_ref[0]
    grads = [grad_ref[0, :, pl.ds(h * HEAD, HEAD)] for h in heads]
    raws = [dot(values, grads[h], 1, 1) for h in heads]
    expos = [jnp.exp(scores[h] - jnp.max(scores[h], axis=0, keepdims=True)) for h in heads]
    probs = [expos[h] * (1.0 / jnp.sum(expos[h], axis=0, keepdims=True)) for h in heads]
    halves = [probs[h].astype(BF16) for h in heads]
    centres = [jnp.sum(probs[h] * raws[h], axis=0, keepdims=True) for h in heads]
    sums = [jnp.sum(halves[h].astype(F32) * raws[h], axis=0, keepdims=True) for h in heads]

    for i in range(4, 6):
        copies[i].wait()
    key_grad = jnp.zeros((SEQ, HEAD), F32)
    value_grad = jnp.zeros((SEQ, HEAD), F32)
    head_sums = jnp.zeros((1, 128), F32)
    layer_part = jnp.zeros((1, 1), F32)
    for h in heads:
        head_id = tensor_place * HEADS_HERE + h
        masked = order_ref[0, 0] == head_id
        for m in range(1, MASKED):
            masked = jnp.logical_or(masked, order_ref[0, m] == head_id)
        open_gate = jnp.where(masked, 0.0, head_gate_ref[0, h])
        scaled = (grads[h].astype(F32) * open_gate).astype(BF16)
        score_grad = (probs[h] * (raws[h] - centres[h]) * (open_gate * scale)).astype(BF16)
        key_grad += dot(score_grad, queries[h], 1, 0)
        value_grad += dot(halves[h], scaled, 1, 0)
        head_sum = jnp.sum(sums[h], axis=1, keepdims=True)
        head_sums += jnp.where(lane == h, head_sum, 0.0)
        layer_part += open_gate * head_sum

    head_sum_ref[...] = head_sums
    both = jnp.concatenate([key_grad.astype(BF16), value_grad.astype(BF16)], axis=1)
    share = jnp.broadcast_to(layer_part, (EXTRA, 128))
    high = share.astype(BF16).astype(F32)
    row = lax.broadcasted_iota(jnp.int32, (EXTRA, 128), 0)
    extra = jnp.where(row < EXTRA // 2, high, share - high)
    copies[6].wait()
    copies[7].wait()
    for j in range(BLOCKS):
        span = pl.ds(j * BLOCK, BLOCK)
        weights = jnp.concatenate([kw_ref[0, span], vw_ref[0, span]], axis=1)
        part_ref[j] = jnp.concatenate([dot(weights, both, 1, 1), extra], axis=0).astype(BF16)


def front(order, head_gate, q, k, v, grad, kw, vw):
    vmem = pl.BlockSpec(memory_space=pltpu.VMEM)
    hbm = pl.BlockSpec(memory_space=pltpu.HBM)
    return pl.pallas_call(
        front_kernel,
        name="front",
        out_shape=(
            jax.ShapeDtypeStruct((BLOCKS, BLOCK + EXTRA, SEQ), BF16),
            jax.ShapeDtypeStruct((1, 128), F32),
        ),
        in_specs=[hbm] * 8,
        out_specs=(vmem, vmem),
        scratch_shapes=[
            pltpu.SMEM(order.shape, jnp.int32),
            pltpu.SMEM(head_gate.shape, F32),
            pltpu.VMEM(q.shape, BF16),
            pltpu.VMEM(k.shape, BF16),
            pltpu.VMEM(v.shape, BF16),
            pltpu.VMEM(grad.shape, BF16),
            pltpu.VMEM(kw.shape, BF16),
            pltpu.VMEM(vw.shape, BF16),
            pltpu.SemaphoreType.DMA((8,)),
        ],
        compiler_params=pltpu.CompilerParams(vmem_limit_bytes=58 * MIB),
    )(order, head_gate, q, k, v, grad, kw, vw)


def pair_kernel(own_ref, core_ref, pair_ref):
    row = lax.broadcasted_iota(jnp.int32, own_ref.shape, 0)
    pair_ref[...] = jnp.where(row < EXTRA // 2, own_ref[...], core_ref[...])


def terms_kernel(parts_ref, gates_ref, y_gates_ref, terms_ref, totals_ref, share_ref):
    own = lax.axis_index("core") * 2 + lax.axis_index("yl")
    total = jnp.zeros((BLOCK, SEQ), F32)
    share = jnp.zeros((EXTRA, SEQ), F32)
    for n in range(NEAR):
        term = parts_ref[n].astype(F32)
        for t in range(1, PARTS):
            term += parts_ref[t * NEAR + n].astype(F32)
        apart = own ^ n
        gate = jnp.where(
            apart == 0,
            gates_ref[:1],
            jnp.where(
                apart == 1,
                y_gates_ref[:1],
                jnp.where(apart == 2, gates_ref[EXTRA // 2:][:1], y_gates_ref[EXTRA // 2:][:1]),
            ),
        )
        scaled = term[:BLOCK] * gate
        terms_ref[n] = scaled
        total += scaled
        share += jnp.where(own == n, term[BLOCK:], 0.0)
    totals_ref[...] = total.astype(BF16)
    share_ref[...] = share


def later_kernel(
    terms_ref, far_1, far_2, far_3, own_ref, to_earlier_ref, first_later_ref, second_later_ref
):
    place = lax.axis_index("zh")
    far = far_1[...].astype(F32) + far_2[...].astype(F32) + far_3[...].astype(F32)
    first = terms_ref[0] + terms_ref[2]
    second = terms_ref[1] + terms_ref[3]
    to_later = (far + second, far)
    to_earlier = (far + second + first, far + second)
    for half in range(2):
        own_ref[half] = to_later[half]
        to_earlier_ref[half] = to_earlier[half].astype(BF16)
        for z, ref in ((0, first_later_ref), (1, second_later_ref)):
            ref[half] = jnp.where(place == z, to_later[half], to_earlier[half]).astype(BF16)


def pass_on_kernel(own_ref, step_1, step_2, step_3, sum_ref, passed_ref):
    second_place = lax.axis_index("zh") == 1
    own = own_ref[...]
    got = step_3[...].astype(F32)
    passed_ref[...] = (own + jnp.where(second_place, got, 0.0)).astype(BF16)
    sum_ref[...] = own + got + step_1[...].astype(F32) + step_2[...].astype(F32)


def sums_kernel(terms_ref, sum_ref, step_5, step_6, step_4, sums_ref):
    for half in range(2):
        running = sum_ref[half] + step_5[half].astype(F32)
        running += step_6[half].astype(F32) + step_4[half].astype(F32)
        for n in (2 + half, half):
            running += terms_ref[n]
            sums_ref[n] = running.T.astype(BF16)


def join_kernel(blocks_ref, share_ref, gate_ref, head_sum_ref, out_ref, head_grad_ref, layer_grad_ref):
    head_grad_ref[...] = (gate_ref[:1] * head_sum_ref[...])[:, :HEADS_HERE]
    layer_grad_ref[0] = share_ref[0, 0] + share_ref[EXTRA // 2, 0]
    for n in range(NEAR):
        out_ref[0, :, n * BLOCK:(n + 1) * BLOCK] = blocks_ref[n]


def small(kernel, name, out_shape, out_specs=None):
    vmem = pl.BlockSpec(memory_space=pltpu.VMEM)
    return pl.pallas_call(
        kernel,
        name=name,
        out_shape=out_shape,
        out_specs=vmem if out_specs is None else out_specs,
        compiler_params=pltpu.CompilerParams(vmem_limit_bytes=16 * MIB),
    )


def body(
    queries, keys, values, out_grad, key_weight, value_weight, head_gate, layer_gate, head_order
):
    part, head_sum = front(
        head_order, head_gate, queries, keys, values, out_grad, key_weight, value_weight
    )
    part, layer_gate = lax.optimization_barrier((part, layer_gate))
    parts = lax.all_to_all(part, TENSOR_AXES + NEAR_AXES, 0, 0)
    gate = jnp.broadcast_to(layer_gate[:, None], (EXTRA, SEQ))
    swap = ((0, 1), (1, 0))
    core_gate = lax.ppermute(gate, "core", swap)
    gates = small(pair_kernel, "gate_pair", jax.ShapeDtypeStruct((EXTRA, SEQ), F32))(
        gate, core_gate
    )
    y_gates = lax.ppermute(gates, "yl", swap)
    vmem = pl.BlockSpec(memory_space=pltpu.VMEM)
    terms, totals, share = small(
        terms_kernel,
        "terms",
        (
            jax.ShapeDtypeStruct((NEAR, BLOCK, SEQ), F32),
            jax.ShapeDtypeStruct((BLOCK, SEQ), BF16),
            jax.ShapeDtypeStruct((EXTRA, SEQ), F32),
        ),
        (vmem, vmem, vmem),
    )(parts, gates, y_gates)
    totals = [
        lax.ppermute(totals, "yh", [(f, f - step) for f in range(step, FAR)]) for step in (3, 2, 1)
    ]
    half_pair = (2, BLOCK, SEQ)
    own, to_earlier, first_later, second_later = small(
        later_kernel,
        "later",
        (
            jax.ShapeDtypeStruct(half_pair, F32),
            jax.ShapeDtypeStruct(half_pair, BF16),
            jax.ShapeDtypeStruct(half_pair, BF16),
            jax.ShapeDtypeStruct(half_pair, BF16),
        ),
        (vmem,) * 4,
    )(terms, *totals)
    step_1 = lax.ppermute(to_earlier, "zh", STEP_1)
    step_2 = lax.ppermute(to_earlier, "zh", STEP_2)
    step_3 = lax.ppermute(first_later, "zh", STEP_3)
    own, passed = small(
        pass_on_kernel,
        "pass_on",
        (jax.ShapeDtypeStruct(half_pair, F32), jax.ShapeDtypeStruct(half_pair, BF16)),
        (vmem,) * 2,
    )(own, step_1, step_2, step_3)
    step_5 = lax.ppermute(second_later, "zh", STEP_5)
    step_6 = lax.ppermute(first_later, "zh", STEP_6)
    step_4 = lax.ppermute(passed, "zh", STEP_4)
    sums = small(
        sums_kernel, "sums", jax.ShapeDtypeStruct((NEAR, SEQ, BLOCK), BF16)
    )(terms, own, step_5, step_6, step_4)
    sums = lax.all_to_all(sums, NEAR_AXES, 0, 0)
    input_grad, head_grad, layer_grad = small(
        join_kernel,
        "join",
        (
            jax.ShapeDtypeStruct((1, SEQ, NEAR * BLOCK), BF16),
            jax.ShapeDtypeStruct((1, HEADS_HERE), F32),
            jax.ShapeDtypeStruct((1,), F32),
        ),
        (vmem, vmem, pl.BlockSpec(memory_space=pltpu.SMEM)),
    )(sums, share, gate, head_sum)
    return input_grad, head_grad, layer_grad


def solution(mesh):
    fine = jax.sharding.Mesh(mesh.devices.reshape(MESH_SHAPE), MESH_AXES)
    rows = P(LAYER_AXES, None, TENSOR_AXES)
    heads = P(LAYER_AXES, TENSOR_AXES)
    layers = P(LAYER_AXES)
    return jax.shard_map(
        body,
        mesh=fine,
        in_specs=(rows, rows, rows, rows, rows, rows, heads, layers, P(LAYER_AXES, None)),
        out_specs=(rows, heads, layers),
        check_vma=False,
    )
```

```python
import jax
import jax.numpy as jnp
from jax import lax
from jax.experimental import pallas as pl
from jax.experimental.pallas import tpu as pltpu
from jax.sharding import PartitionSpec as P

HEAD = 128
MASKED = 8
SEQ = 128
WIDTH = 4096
HEADS_HERE = 4
PARTS = 8
NEAR = 4
BLOCKS = PARTS * NEAR
BLOCK = WIDTH // BLOCKS
EXTRA = 8
FAR = 4
STEP_1 = ((3, 0), (2, 1))
STEP_2 = ((2, 0), (3, 1))
STEP_3 = ((0, 1), (1, 0))
STEP_4 = ((1, 2), (2, 3))
STEP_5 = ((3, 2), (1, 3))
STEP_6 = ((0, 3),)

MESH_AXES = ("yh", "yl", "zh", "core", "zl", "x")
MESH_SHAPE = (4, 2, 4, 2, 2, 4)
LAYER_AXES = ("yh", "yl", "zh", "core")
TENSOR_AXES = ("zl", "x")
NEAR_AXES = ("core", "yl")

F32 = jnp.float32
BF16 = jnp.bfloat16
MIB = 1024 * 1024


def dot(a, b, a_dim, b_dim):
    return lax.dot_general(a, b, (((a_dim,), (b_dim,)), ((), ())), preferred_element_type=F32)


def front_kernel(
    order_hbm, head_gate_hbm, q_hbm, k_hbm, v_hbm, grad_hbm, kw_hbm, vw_hbm,
    part_ref, head_sum_ref,
    order_ref, head_gate_ref, q_ref, k_ref, v_ref, grad_ref, kw_ref, vw_ref, sems,
):
    pairs = (
        (k_hbm, k_ref), (q_hbm, q_ref), (v_hbm, v_ref), (grad_hbm, grad_ref),
        (order_hbm, order_ref), (head_gate_hbm, head_gate_ref),
        (kw_hbm, kw_ref), (vw_hbm, vw_ref),
    )
    copies = [
        pltpu.make_async_copy(source, target, sems.at[i])
        for i, (source, target) in enumerate(pairs)
    ]
    for copy in copies:
        copy.start()

    tensor_place = lax.axis_index("zl") * 4 + lax.axis_index("x")
    scale = HEAD ** (-0.5)
    heads = range(HEADS_HERE)
    key_at = lax.broadcasted_iota(jnp.int32, (SEQ, SEQ), 0)
    query_at = lax.broadcasted_iota(jnp.int32, (SEQ, SEQ), 1)
    seen = key_at <= query_at
    lane = lax.broadcasted_iota(jnp.int32, (1, 128), 1)

    copies[0].wait()
    copies[1].wait()
    keys = k_ref[0]
    queries = [q_ref[0, :, pl.ds(h * HEAD, HEAD)] for h in heads]
    scores = [jnp.where(seen, dot(keys, queries[h], 1, 1) * scale, -1e30) for h in heads]
    copies[2].wait()
    copies[3].wait()
    values = v_ref[0]
    grads = [grad_ref[0, :, pl.ds(h * HEAD, HEAD)] for h in heads]
    raws = [dot(values, grads[h], 1, 1) for h in heads]
    expos = [jnp.exp(scores[h] - jnp.max(scores[h], axis=0, keepdims=True)) for h in heads]
    probs = [expos[h] * (1.0 / jnp.sum(expos[h], axis=0, keepdims=True)) for h in heads]
    halves = [probs[h].astype(BF16) for h in heads]
    centres = [jnp.sum(probs[h] * raws[h], axis=0, keepdims=True) for h in heads]
    sums = [jnp.sum(halves[h].astype(F32) * raws[h], axis=0, keepdims=True) for h in heads]

    for i in range(4, 6):
        copies[i].wait()
    key_grad = jnp.zeros((SEQ, HEAD), F32)
    value_grad = jnp.zeros((SEQ, HEAD), F32)
    head_sums = jnp.zeros((1, 128), F32)
    layer_part = jnp.zeros((1, 1), F32)
    for h in heads:
        head_id = tensor_place * HEADS_HERE + h
        masked = order_ref[0, 0] == head_id
        for m in range(1, MASKED):
            masked = jnp.logical_or(masked, order_ref[0, m] == head_id)
        open_gate = jnp.where(masked, 0.0, head_gate_ref[0, h])
        scaled = (grads[h].astype(F32) * open_gate).astype(BF16)
        score_grad = (probs[h] * (raws[h] - centres[h]) * (open_gate * scale)).astype(BF16)
        key_grad += dot(score_grad, queries[h], 1, 0)
        value_grad += dot(halves[h], scaled, 1, 0)
        head_sum = jnp.sum(sums[h], axis=1, keepdims=True)
        head_sums += jnp.where(lane == h, head_sum, 0.0)
        layer_part += open_gate * head_sum

    head_sum_ref[...] = head_sums
    both = jnp.concatenate([key_grad.astype(BF16), value_grad.astype(BF16)], axis=1)
    share = jnp.broadcast_to(layer_part, (EXTRA, 128))
    high = share.astype(BF16).astype(F32)
    row = lax.broadcasted_iota(jnp.int32, (EXTRA, 128), 0)
    extra = jnp.where(row < EXTRA // 2, high, share - high)
    copies[6].wait()
    copies[7].wait()
    for j in range(BLOCKS):
        span = pl.ds(j * BLOCK, BLOCK)
        weights = jnp.concatenate([kw_ref[0, span], vw_ref[0, span]], axis=1)
        part_ref[j] = jnp.concatenate([dot(weights, both, 1, 1), extra], axis=0).astype(BF16)


def front(order, head_gate, q, k, v, grad, kw, vw):
    vmem = pl.BlockSpec(memory_space=pltpu.VMEM)
    hbm = pl.BlockSpec(memory_space=pltpu.HBM)
    return pl.pallas_call(
        front_kernel,
        name="front",
        out_shape=(
            jax.ShapeDtypeStruct((BLOCKS, BLOCK + EXTRA, SEQ), BF16),
            jax.ShapeDtypeStruct((1, 128), F32),
        ),
        in_specs=[hbm] * 8,
        out_specs=(vmem, vmem),
        scratch_shapes=[
            pltpu.SMEM(order.shape, jnp.int32),
            pltpu.SMEM(head_gate.shape, F32),
            pltpu.VMEM(q.shape, BF16),
            pltpu.VMEM(k.shape, BF16),
            pltpu.VMEM(v.shape, BF16),
            pltpu.VMEM(grad.shape, BF16),
            pltpu.VMEM(kw.shape, BF16),
            pltpu.VMEM(vw.shape, BF16),
            pltpu.SemaphoreType.DMA((8,)),
        ],
        compiler_params=pltpu.CompilerParams(vmem_limit_bytes=24 * MIB),
    )(*[
        pltpu.with_memory_space_constraint(operand, pltpu.HBM)
        for operand in (order, head_gate, q, k, v, grad, kw, vw)
    ])


def pair_kernel(own_ref, core_ref, pair_ref):
    row = lax.broadcasted_iota(jnp.int32, own_ref.shape, 0)
    pair_ref[...] = jnp.where(row < EXTRA // 2, own_ref[...], core_ref[...])


def terms_kernel(parts_ref, gates_ref, y_gates_ref, terms_ref, totals_ref, share_ref):
    own = lax.axis_index("core") * 2 + lax.axis_index("yl")
    total = jnp.zeros((BLOCK, SEQ), F32)
    share = jnp.zeros((EXTRA, SEQ), F32)
    for n in range(NEAR):
        term = parts_ref[n].astype(F32)
        for t in range(1, PARTS):
            term += parts_ref[t * NEAR + n].astype(F32)
        apart = own ^ n
        gate = jnp.where(
            apart == 0,
            gates_ref[:1],
            jnp.where(
                apart == 1,
                y_gates_ref[:1],
                jnp.where(apart == 2, gates_ref[EXTRA // 2:][:1], y_gates_ref[EXTRA // 2:][:1]),
            ),
        )
        scaled = term[:BLOCK] * gate
        terms_ref[n] = scaled
        total += scaled
        share += jnp.where(own == n, term[BLOCK:], 0.0)
    totals_ref[...] = total.astype(BF16)
    share_ref[...] = share


def later_kernel(
    terms_ref, far_1, far_2, far_3, own_ref, to_earlier_ref, first_later_ref, second_later_ref
):
    place = lax.axis_index("zh")
    far = far_1[...].astype(F32) + far_2[...].astype(F32) + far_3[...].astype(F32)
    first = terms_ref[0] + terms_ref[2]
    second = terms_ref[1] + terms_ref[3]
    to_later = (far + second, far)
    to_earlier = (far + second + first, far + second)
    for half in range(2):
        own_ref[half] = to_later[half]
        to_earlier_ref[half] = to_earlier[half].astype(BF16)
        for z, ref in ((0, first_later_ref), (1, second_later_ref)):
            ref[half] = jnp.where(place == z, to_later[half], to_earlier[half]).astype(BF16)


def pass_on_kernel(own_ref, step_1, step_2, step_3, sum_ref, passed_ref):
    second_place = lax.axis_index("zh") == 1
    own = own_ref[...]
    got = step_3[...].astype(F32)
    passed_ref[...] = (own + jnp.where(second_place, got, 0.0)).astype(BF16)
    sum_ref[...] = own + got + step_1[...].astype(F32) + step_2[...].astype(F32)


def sums_kernel(terms_ref, sum_ref, step_5, step_6, step_4, sums_ref):
    for half in range(2):
        running = sum_ref[half] + step_5[half].astype(F32)
        running += step_6[half].astype(F32) + step_4[half].astype(F32)
        for n in (2 + half, half):
            running += terms_ref[n]
            sums_ref[n] = running.T.astype(BF16)


def join_kernel(blocks_ref, share_ref, gate_ref, head_sum_ref, out_ref, head_grad_ref, layer_grad_ref):
    head_grad_ref[...] = (gate_ref[:1] * head_sum_ref[...])[:, :HEADS_HERE]
    layer_grad_ref[0] = share_ref[0, 0] + share_ref[EXTRA // 2, 0]
    for n in range(NEAR):
        out_ref[0, :, n * BLOCK:(n + 1) * BLOCK] = blocks_ref[n]


def small(kernel, name, out_shape, out_specs=None):
    vmem = pl.BlockSpec(memory_space=pltpu.VMEM)
    return pl.pallas_call(
        kernel,
        name=name,
        out_shape=out_shape,
        out_specs=vmem if out_specs is None else out_specs,
        compiler_params=pltpu.CompilerParams(vmem_limit_bytes=16 * MIB),
    )


def body(
    queries, keys, values, out_grad, key_weight, value_weight, head_gate, layer_gate, head_order
):
    part, head_sum = front(
        head_order, head_gate, queries, keys, values, out_grad, key_weight, value_weight
    )
    part, layer_gate = lax.optimization_barrier((part, layer_gate))
    parts = lax.all_to_all(part, TENSOR_AXES + NEAR_AXES, 0, 0)
    gate = jnp.broadcast_to(layer_gate[:, None], (EXTRA, SEQ))
    swap = ((0, 1), (1, 0))
    core_gate = lax.ppermute(gate, "core", swap)
    gates = small(pair_kernel, "gate_pair", jax.ShapeDtypeStruct((EXTRA, SEQ), F32))(
        gate, core_gate
    )
    y_gates = lax.ppermute(gates, "yl", swap)
    vmem = pl.BlockSpec(memory_space=pltpu.VMEM)
    terms, totals, share = small(
        terms_kernel,
        "terms",
        (
            jax.ShapeDtypeStruct((NEAR, BLOCK, SEQ), F32),
            jax.ShapeDtypeStruct((BLOCK, SEQ), BF16),
            jax.ShapeDtypeStruct((EXTRA, SEQ), F32),
        ),
        (vmem, vmem, vmem),
    )(parts, gates, y_gates)
    totals = [
        lax.ppermute(totals, "yh", [(f, f - step) for f in range(step, FAR)]) for step in (3, 2, 1)
    ]
    half_pair = (2, BLOCK, SEQ)
    own, to_earlier, first_later, second_later = small(
        later_kernel,
        "later",
        (
            jax.ShapeDtypeStruct(half_pair, F32),
            jax.ShapeDtypeStruct(half_pair, BF16),
            jax.ShapeDtypeStruct(half_pair, BF16),
            jax.ShapeDtypeStruct(half_pair, BF16),
        ),
        (vmem,) * 4,
    )(terms, *totals)
    step_1 = lax.ppermute(to_earlier, "zh", STEP_1)
    step_2 = lax.ppermute(to_earlier, "zh", STEP_2)
    step_3 = lax.ppermute(first_later, "zh", STEP_3)
    own, passed = small(
        pass_on_kernel,
        "pass_on",
        (jax.ShapeDtypeStruct(half_pair, F32), jax.ShapeDtypeStruct(half_pair, BF16)),
        (vmem,) * 2,
    )(own, step_1, step_2, step_3)
    step_5 = lax.ppermute(second_later, "zh", STEP_5)
    step_6 = lax.ppermute(first_later, "zh", STEP_6)
    step_4 = lax.ppermute(passed, "zh", STEP_4)
    sums = small(
        sums_kernel, "sums", jax.ShapeDtypeStruct((NEAR, SEQ, BLOCK), BF16)
    )(terms, own, step_5, step_6, step_4)
    sums = lax.all_to_all(sums, NEAR_AXES, 0, 0)
    input_grad, head_grad, layer_grad = small(
        join_kernel,
        "join",
        (
            jax.ShapeDtypeStruct((1, SEQ, NEAR * BLOCK), BF16),
            jax.ShapeDtypeStruct((1, HEADS_HERE), F32),
            jax.ShapeDtypeStruct((1,), F32),
        ),
        (vmem, vmem, pl.BlockSpec(memory_space=pltpu.SMEM)),
    )(sums, share, gate, head_sum)
    return input_grad, head_grad, layer_grad


def solution(mesh):
    fine = jax.sharding.Mesh(mesh.devices.reshape(MESH_SHAPE), MESH_AXES)
    rows = P(LAYER_AXES, None, TENSOR_AXES)
    heads = P(LAYER_AXES, TENSOR_AXES)
    layers = P(LAYER_AXES)
    return jax.shard_map(
        body,
        mesh=fine,
        in_specs=(rows, rows, rows, rows, rows, rows, heads, layers, P(LAYER_AXES, None)),
        out_specs=(rows, heads, layers),
        check_vma=False,
    )
```
